512 devices in a mesh: section: 8 (over y, core), tensor: 64 (over x, z).
Axes of the slice: x: 4, y: 4, z: 16, core: 2. Of those that a mesh axis runs over, the one named last changes fastest.
Arguments:
- hidden: bfloat16 [2048, 8192], P('section', 'tensor'), may hold values from -6 to 6
- arriving: bfloat16 [256, 8192], P(None, 'tensor'), may hold values from -6 to 6
- ids: int32 [9, 256, 1], replicated, may hold values from 0 to 63; in each aligned block of 256 rows (0 to 255, 256 to 511, ..., all dimensions but the last counted through in order) at most 16 rows name the same one
- adapter_slot: int32 [64], replicated, may hold values from 0 to 63, each once
- base_matrix: bfloat16 [8, 8192, 8192], P('section', None, 'tensor'), may hold values from -0.0625 to 0.0625
- adapter_down: bfloat16 [8, 64, 8192, 64], P('section', 'tensor'), may hold values from -0.0625 to 0.0625
- adapter_up: bfloat16 [8, 64, 64, 8192], P('section', 'tensor'), may hold values from -0.75 to 0.75
Outputs:
- outputs: bfloat16 [2, 2048, 8192], P(None, 'section', 'tensor')
The draws below stay inside these ranges and needn't reach their ends.
Inputs may be any that keep to these rules, and one draw needn't show every extreme that they name: `ids`: within each microbatch of 256 requests no adapter is named by more than 16 requests, and this bound is reached. A permutation: adapter a sits in store slot adapter_slot[a], on tensor device adapter_slot[a] of its section.
All inputs are finite; a program needn't handle non-finite values.
Results may differ from the reference program's by a relative error of at most 0.012.
Values may be sent and summed in bfloat16 or wider, within the bound.
A program may use at most 64 MiB of HBM per device.

```python
import math
import jax
import jax.numpy as jnp
import numpy as np

MODEL_WIDTH = 8192
ADAPTER_RANK = 64
MB = 256
CAP = 16
TICKS = 2
ADAPTER_COUNT = 64
SECTION_TOTAL = 8
MICRO = 9


def level_of(key, extent, split, low, top_value):
    def one(axis_at, shards_of):
        steps = jax.random.uniform(jax.random.fold_in(jax.random.fold_in(key, 6), axis_at), (shards_of,), jnp.float32, low / len(split), top_value / len(split))
        return jnp.repeat(jnp.exp(steps), extent[axis_at] // shards_of).reshape((-1,) + (1,) * (len(extent) - axis_at - 1))

    gain = one(*split[0])
    for cut in split[1:]:
        gain = gain * one(*cut)
    return gain


def assign_block(key, own, number, rows, number_of, top, most, lean):
    order = jax.random.permutation(key, number_of)
    crowded, usual = portions_of(number_of, rows * top, most, lean, True), portions_of(number_of, rows * top, most, lean, False)
    places = jnp.arange(number_of)

    def named(lengths, turn):
        used = int((lengths > 0).sum())
        fixed = max(1, used // 4)
        passed = fixed + (places - fixed + turn * (used - fixed)) % max(1, number_of - fixed)
        return jnp.zeros((number_of,), jnp.int32).at[order[jnp.where(places < fixed, places, passed)]].set(jnp.asarray(lengths, jnp.int32))

    lengths = jnp.where(number % 4 == 0, named(crowded, number // 4), named(usual, number - number // 4 - 1))
    mixed = jax.random.permutation(jax.random.fold_in(own, 3), number_of)
    giver, receiver = mixed[0:number_of // 2 * 2:2], mixed[1:number_of // 2 * 2:2]
    room = jnp.minimum(lengths[giver] - 1, most - lengths[receiver]) // 2
    room = jnp.where((giver == order[0]) | (receiver == order[0]) | (lengths[receiver] == 0), 0, jnp.maximum(room, 0))
    passed = jax.random.randint(jax.random.fold_in(own, 4), (number_of // 2,), 0, 1 << 20) % (room + 1)
    lengths = lengths.at[giver].add(-passed).at[receiver].add(passed)
    labels = jnp.searchsorted(jnp.cumsum(lengths), jnp.arange(rows * top), side="right").astype(jnp.int32)
    listing = labels.reshape(top, rows).T
    listing = listing[jax.random.permutation(jax.random.fold_in(own, 1), rows)]
    turn = jax.random.randint(jax.random.fold_in(own, 2), (rows, 1), 0, top)
    return jnp.take_along_axis(listing, (jnp.arange(top)[None, :] + turn) % top, axis=1)


def portions_of(count, total, limit, slope, full):
    loads = [(1 << 20) // math.isqrt(standing ** slope) + 1 for standing in range(1, count + 1)]
    largest = limit if full else min(limit, max(-(-total // count), total * loads[0] // sum(loads)))
    least = 1 if total - largest >= count - 1 else 0
    counts, rest = [largest] + [least] * (count - 1), total - largest - least * (count - 1)
    while rest > 0:
        movable = [i for i in range(1, count) if counts[i] < largest] or [i for i in range(1, count) if counts[i] < limit]
        whole, remaining = sum([loads[i] for i in movable]), rest
        for i in movable:
            more = min(limit - counts[i], max(1, remaining * loads[i] // whole), rest)
            counts[i] = counts[i] + more
            rest = rest - more
    return np.array(counts)


def normal_values(stream_key, dims, deviation, limit, pieces=(), kind=jnp.bfloat16):
    result = jax.random.normal(stream_key, dims, jnp.float32) * deviation
    if len(pieces) > 0:
        result = level_of(stream_key, dims, pieces, -0.22, 0.18) * result
    return jnp.clip(result, min=-limit, max=limit).astype(kind)


def setup_inputs(seed: int = 0) -> dict:
    keys = jax.random.split(jax.random.key(seed), 8)
    hidden = normal_values(keys[0], (SECTION_TOTAL * MB, MODEL_WIDTH), 1.0, 6.0, ((0, 8), (1, 64)))
    arriving = normal_values(keys[1], ((TICKS - 1) * MB, MODEL_WIDTH), 1.0, 6.0, ((1, 64),))
    ids_keys = jax.random.split(jax.random.fold_in(keys[2], 1), MICRO * MB // MB)
    ids_turns = jax.random.permutation(jax.random.fold_in(keys[2], 3), MICRO * MB // MB)
    ids = jax.vmap(lambda own, number: assign_block(jax.random.fold_in(keys[2], 2), own, number, MB, ADAPTER_COUNT, 1, CAP, 2))(ids_keys, ids_turns).reshape((MICRO, MB, 1))
    adapter_slot = jax.random.permutation(keys[3], ADAPTER_COUNT).astype(jnp.int32)
    base_matrix = normal_values(keys[4], (SECTION_TOTAL, MODEL_WIDTH, MODEL_WIDTH), MODEL_WIDTH ** -0.5, 0.0625, ((0, 8), (2, 64)))
    adapter_down = normal_values(keys[5], (SECTION_TOTAL, ADAPTER_COUNT, MODEL_WIDTH, ADAPTER_RANK), MODEL_WIDTH ** -0.5, 0.0625, ((0, 8), (1, 64)))
    adapter_up = normal_values(keys[6], (SECTION_TOTAL, ADAPTER_COUNT, ADAPTER_RANK, MODEL_WIDTH), ADAPTER_RANK ** -0.5, 0.75, ((0, 8), (1, 64)))
    return {"hidden": hidden, "arriving": arriving, "ids": ids, "adapter_slot": adapter_slot, "base_matrix": base_matrix, "adapter_down": adapter_down, "adapter_up": adapter_up}


def run_section_layer(input_rows, row_ids, adapter_slot, weight, a_store, up_store):
    slot_ids = adapter_slot[row_ids]
    adapter_ids, hidden_width, adapter_rank_size = a_store.shape
    row_count = input_rows.shape[0]
    down_flat = jnp.transpose(a_store, (1, 0, 2)).reshape(hidden_width, adapter_ids * adapter_rank_size)
    low_rank = jnp.dot(input_rows, down_flat, preferred_element_type=jnp.float32).reshape(row_count, adapter_ids, adapter_rank_size)
    onehot = slot_ids[:, None] == jnp.arange(adapter_ids, dtype=jnp.int32)[None, :]
    chosen = jnp.sum(jnp.where(onehot[:, :, None], low_rank, jnp.zeros((), jnp.float32)), axis=1).astype(jnp.bfloat16)
    expanded_rows = jnp.where(onehot[:, :, None], chosen[:, None, :], jnp.zeros((), jnp.bfloat16)).reshape(row_count, adapter_ids * adapter_rank_size)
    adapter_product = jnp.dot(expanded_rows, up_store.reshape(adapter_ids * adapter_rank_size, hidden_width), preferred_element_type=jnp.float32).astype(jnp.bfloat16)
    base_product = jnp.dot(input_rows, weight, preferred_element_type=jnp.float32)
    return (input_rows.astype(jnp.float32) + base_product + adapter_product.astype(jnp.float32)).astype(jnp.bfloat16)


def reference(hidden, arriving, ids, adapter_slot, base_matrix, adapter_down, adapter_up):
    current_state = [hidden[section_position * MB:(section_position + 1) * MB] for section_position in range(SECTION_TOTAL)]
    results = []
    for step_index in range(TICKS):
        section_results = []
        for section_position in range(SECTION_TOTAL):
            if section_position >= step_index:
                microbatch_index = section_position - step_index
            else:
                microbatch_index = SECTION_TOTAL + step_index - 1 - section_position
            section_results.append(run_section_layer(current_state[section_position], ids[microbatch_index, :, 0], adapter_slot, base_matrix[section_position], adapter_down[section_position], adapter_up[section_position]))
        results.append(jnp.concatenate(section_results, 0))
        if step_index + 1 < TICKS:
            current_state = [arriving[step_index * MB:(step_index + 1) * MB]] + section_results[:-1]
    return jnp.stack(results, 0)
```

```python
import functools

import jax
import jax.numpy as jnp
from jax import lax
from jax.experimental import pallas as pl
from jax.experimental.pallas import tpu as pltpu
from jax.sharding import PartitionSpec as P

TICKS = 2
CAP = 16
NX = 4
XFIRST = 96
MESH = pl.DeviceIdType.MESH
BF16, F32 = jnp.bfloat16, jnp.float32


def kernel(nz, hidden, arriving, ids, aslot, w_any, d_any, u_any, out, xa, xb, w, d, u, acc, pick, place, lsend, lrecv,
           ssem, rsem, lsem, lora_ssem, lora_rsem):
    nt = NX * nz
    half = nz // 2
    rows = out.shape[1]
    ra, rb = XFIRST, rows - XFIRST
    ha, hb = ra // 2, rb // 2
    rank = u.shape[0]
    section = lax.axis_index("section")
    sections = lax.axis_size("section")
    me = lax.axis_index("tensor")
    x, z = me // nz, me % nz
    x_next, x_back = ((x + 1) % NX) * nz + z, ((x + NX - 1) % NX) * nz + z
    z_next, z_back = x * nz + (z + 1) % nz, x * nz + (z + nz - 1) % nz
    s_next, s_back = (section + 1) % sections, (section + sections - 1) % sections
    x_to, z_to = (x_next, x_back), (z_next, z_back)

    locals_ = [
        pltpu.make_async_copy(hidden.at[0:ra], xa.at[0, 0, 0], lsem.at[0]),
        pltpu.make_async_copy(hidden.at[ra:rows], xb.at[0, 0, 0], lsem.at[1]),
        pltpu.make_async_copy(w_any, w, lsem.at[2]),
        pltpu.make_async_copy(d_any, d, lsem.at[3]),
        pltpu.make_async_copy(u_any, u, lsem.at[4]),
    ]
    entry = [
        pltpu.make_async_copy(arriving.at[0:ra], xa.at[1, 0, 0], lsem.at[5]),
        pltpu.make_async_copy(arriving.at[ra:rows], xb.at[1, 0, 0], lsem.at[6]),
    ]
    for c in locals_:
        c.start()

    @pl.when(section == 0)
    def _():
        for c in entry:
            c.start()

    barrier = pltpu.get_barrier_semaphore()
    for target in ((section, x_next), (section, x_back), (section, z_next), (section, z_back), (s_next, me), (s_back, me)):
        pl.semaphore_signal(barrier, inc=1, device_id=target, device_id_type=MESH)
    pl.semaphore_wait(barrier, 6)

    sent = []
    n = half + 1
    BZ, AZ, BX, BN, AX, AN, SH = 0, 2 * n, 6 * n, 8 * n, 10 * n, 10 * n + 2, 10 * n + 4

    def send(tick, sem, src, dst, to, where=None):
        c = pltpu.make_async_remote_copy(
            src_ref=src, dst_ref=dst, send_sem=ssem.at[tick, sem], recv_sem=rsem.at[tick, sem],
            device_id=(section, to) if where is None else where, device_id_type=MESH)
        c.start()
        sent.append(c)
        return c

    def slot_of(direction, k):
        return nz - 1 if k == half else 2 * k - 1 + direction

    def source(x_rel, slot):
        sx = (x + (0, NX - 1, 1, 2)[x_rel]) % NX
        if slot == 0:
            sz = z
        elif slot == nz - 1:
            sz = (z + half) % nz
        else:
            k = (slot + 1) // 2
            sz = (z + (nz - k if slot % 2 == 1 else k)) % nz
        return pl.multiple_of((sx * nz + sz) * 128, 128)

    def accumulate(first, count, chunks):
        lhs = jnp.concatenate([c for c, _ in chunks], axis=1)
        base = jnp.concatenate([w[pl.ds(o, 128), :] for _, o in chunks], axis=0)
        down = jnp.concatenate([d[:, pl.ds(o, 128)] for _, o in chunks], axis=1)
        acc[first:first + count, 0:128] += jnp.dot(lhs, base, preferred_element_type=F32)
        acc[first:first + count, 128:128 + rank] += lax.dot_general(lhs, down, (((1,), (1,)), ((), ())), preferred_element_type=F32)

    def compute_a(tick, slots):
        accumulate(0, ra, [(xa[tick, s, r], source(r, s)) for s in slots for r in range(NX)])

    def compute_b(tick, slots):
        accumulate(ra, rb, [(xb[tick, r, s], source(r, s)) for s in slots for r in range(NX)])

    def positions(tick):
        micro = jnp.where(section >= tick, section - tick, sections + tick - 1 - section)
        id_row = ids[micro].astype(F32)
        i0 = lax.broadcasted_iota(jnp.int32, (rows, rows), 0)
        i1 = lax.broadcasted_iota(jnp.int32, (rows, rows), 1)
        id_col = jnp.sum(jnp.where(i0 == i1, id_row, 0.0), axis=1, keepdims=True)
        same = id_col == id_row
        rank_row = jnp.sum(jnp.where(same & (i0 < i1), 1.0, 0.0), axis=0, keepdims=True)
        rank_col = jnp.sum(jnp.where(same & (i1 < i0), 1.0, 0.0), axis=1, keepdims=True)
        named = lax.broadcasted_iota(jnp.int32, (rows, nt), 1).astype(F32) == id_col
        slot_col = jnp.sum(jnp.where(named, aslot[...].astype(F32), 0.0), axis=1, keepdims=True)
        slot_row = jnp.sum(jnp.where(i0 == i1, slot_col, 0.0), axis=0, keepdims=True)
        j = lax.broadcasted_iota(jnp.int32, (CAP, rows), 0).astype(F32)
        pick[tick] = ((slot_row == me.astype(F32)) & (rank_row == j)).astype(BF16)
        q = lax.broadcasted_iota(jnp.int32, (rows, nt * CAP), 1).astype(F32)
        place[tick] = (slot_col * CAP + rank_col == q).astype(BF16)

    groups = ((0, 1), (1, 3))

    def tick_work(tick):
        bz, az, bx, bn = {}, {}, {}, {}
        acc[...] = jnp.zeros_like(acc)
        ax = [send(tick, AX + i, xa.at[tick, 0, 0], xa.at[tick, 0, 1 + i], x_to[i]) for i in (0, 1)]

        def send_bz(k):
            for i in (0, 1):
                s0, s1 = (0 if k == 1 else slot_of(i, k - 1)), slot_of(i, k)
                part = pl.ds(i * hb, hb) if k == half else pl.ds(0, rb)
                bz[i, k] = send(tick, BZ + i * n + k, xb.at[tick, 0, s0, part], xb.at[tick, 0, s1, part], z_to[i])

        def send_az(k, g):
            start, count = groups[g]
            for i in (0, 1):
                s0, s1 = (0 if k == 1 else slot_of(i, k - 1)), slot_of(i, k)
                if k == half:
                    start, count = 2 * i, 2
                part = pl.ds(start, count)
                az[i, k, g] = send(tick, AZ + (i * n + k) * 2 + g, xa.at[tick, s0, part], xa.at[tick, s1, part], z_to[i])

        def span(k):
            return pl.ds(0, 1) if k == 0 else pl.ds(nz - 1, 1) if k == half else pl.ds(2 * k - 1, 2)

        def slots(k):
            return (0,) if k == 0 else (nz - 1,) if k == half else (2 * k - 1, 2 * k)

        def send_bx(k):
            for i in (0, 1):
                bx[i, k] = send(tick, BX + i * n + k, xb.at[tick, 0, span(k)], xb.at[tick, 1 + i, span(k)], x_to[i])

        def send_bn(k):
            for i in (0, 1):
                bx[i, k].wait_recv()
            for i in (0, 1):
                if k in (0, half):
                    s, part = slots(k)[0], pl.ds(i * hb, hb)
                else:
                    s, part = slots(k)[i], pl.ds(0, rb)
                bn[i, k] = send(tick, BN + i * n + k, xb.at[tick, 1 + i, s, part], xb.at[tick, 3, s, part], x_to[i])

        def finish_b(k):
            for i in (0, 1):
                bn[i, k].wait_recv()
            compute_b(tick, slots(k))

        send_bz(1)
        send_az(1, 0)
        send_bx(0)
        if tick == 0:
            positions(0)
        for c in ax:
            c.wait_recv()
        an = [send(tick, AN + i, xa.at[tick, 0, 1 + i, pl.ds(i * ha, ha)], xa.at[tick, 0, 3, pl.ds(i * ha, ha)], x_to[i]) for i in (0, 1)]
        for c in an:
            c.wait_recv()
        send_az(1, 1)
        if tick == 0:
            positions(1)
            for c in locals_[2:]:
                c.wait()
        compute_a(tick, (0,))
        for k in range(1, half + 1):
            for i in (0, 1):
                bz[i, k].wait_recv()
            if k < half:
                send_bz(k + 1)
            send_bx(k)
            send_bn(k - 1)
            for g in ((0,) if k == half else (0, 1)):
                for i in (0, 1):
                    az[i, k, g].wait_recv()
                if k + 1 < half:
                    send_az(k + 1, g)
            if k + 1 == half:
                send_az(half, 0)
            compute_a(tick, slots(k))
            if k >= 2:
                finish_b(k - 2)
        send_bn(half)
        finish_b(half - 1)
        finish_b(half)

        low = jnp.dot(pick[tick], acc[:, 128:128 + rank].astype(BF16), preferred_element_type=F32).astype(BF16)
        wide = 512
        per = wide // 128

        def widen(i, carry):
            at = pl.multiple_of(i * wide, wide)
            part = jnp.dot(low, u[:, pl.ds(at, wide)], preferred_element_type=F32).astype(BF16)
            for j in range(per):
                lsend[i * per + j] = part[:, j * 128:(j + 1) * 128]
            return carry

        lax.fori_loop(0, nt // per, widen, 0)

        def spread(i, carry):
            to = (me + i) % nt
            pltpu.make_async_remote_copy(
                src_ref=lsend.at[to], dst_ref=lrecv.at[tick, me], send_sem=lora_ssem.at[tick], recv_sem=lora_rsem.at[tick],
                device_id=(section, to), device_id_type=MESH).start()
            return carry

        lax.fori_loop(1, nt, spread, 0)
        own = pltpu.make_async_copy(lsend.at[me], lrecv.at[tick, me], lsem.at[7])
        own.start()
        own.wait()
        others = pltpu.make_async_remote_copy(
            src_ref=lsend.at[0:nt - 1], dst_ref=lrecv.at[tick, 0:nt - 1], send_sem=lora_ssem.at[tick], recv_sem=lora_rsem.at[tick],
            device_id=(section, x_next), device_id_type=MESH)
        others.wait_recv()
        lora = jnp.dot(place[tick], lrecv[tick].reshape(nt * CAP, 128), preferred_element_type=F32)
        held = jnp.concatenate([xa[tick, 0, 0], xb[tick, 0, 0]], axis=0).astype(F32)
        out[tick] = (held + acc[:, 0:128] + lora).astype(BF16)
        others.wait_send()

    for c in locals_[:2]:
        c.wait()
    tick_work(0)

    shift = [
        pltpu.make_async_remote_copy(
            src_ref=out.at[0, first:first + count], dst_ref=dst, send_sem=ssem.at[0, SH + i], recv_sem=rsem.at[0, SH + i],
            device_id=(s_next, me), device_id_type=MESH)
        for i, (first, count, dst) in enumerate(((0, ra, xa.at[1, 0, 0]), (ra, rb, xb.at[1, 0, 0])))
    ]

    @pl.when(section + 1 < sections)
    def _():
        for c in shift:
            c.start()

    @pl.when(section > 0)
    def _():
        for c in shift:
            c.wait_recv()

    @pl.when(section == 0)
    def _():
        for c in entry:
            c.wait()

    tick_work(1)

    @pl.when(section + 1 < sections)
    def _():
        for c in shift:
            c.wait_send()

    for c in sent:
        c.wait_send()


def local(hidden, arriving, ids, adapter_slot, base_matrix, adapter_down, adapter_up):
    rows, cols = hidden.shape
    width = base_matrix.shape[1]
    rank = adapter_down.shape[3]
    nt = lax.axis_size("tensor")
    nz = nt // NX
    sems = 10 * (nz // 2 + 1) + 6
    vmem, hbm = pl.BlockSpec(memory_space=pltpu.VMEM), pl.BlockSpec(memory_space=pl.ANY)
    return pl.pallas_call(
        functools.partial(kernel, nz),
        out_shape=jax.ShapeDtypeStruct((TICKS, rows, cols), BF16),
        in_specs=[hbm, hbm, vmem, vmem, hbm, hbm, hbm],
        out_specs=vmem,
        scratch_shapes=[
            pltpu.VMEM((TICKS, nz, NX, XFIRST, cols), BF16),
            pltpu.VMEM((TICKS, NX, nz, rows - XFIRST, cols), BF16),
            pltpu.VMEM((width, cols), BF16),
            pltpu.VMEM((rank, width), BF16),
            pltpu.VMEM((rank, width), BF16),
            pltpu.VMEM((rows, cols + rank), F32),
            pltpu.VMEM((TICKS, CAP, rows), BF16),
            pltpu.VMEM((TICKS, rows, nt * CAP), BF16),
            pltpu.VMEM((nt, CAP, cols), BF16),
            pltpu.VMEM((TICKS, nt, CAP, cols), BF16),
            pltpu.SemaphoreType.DMA((TICKS, sems)),
            pltpu.SemaphoreType.DMA((TICKS, sems)),
            pltpu.SemaphoreType.DMA((8,)),
            pltpu.SemaphoreType.DMA((TICKS,)),
            pltpu.SemaphoreType.DMA((TICKS,)),
        ],
        compiler_params=pltpu.CompilerParams(collective_id=0, has_side_effects=True, vmem_limit_bytes=40 * 1024 * 1024),
    )(hidden, arriving, ids.reshape(ids.shape[0], 1, ids.shape[1]), adapter_slot.reshape(1, nt), base_matrix[0], adapter_down[0, 0].T, adapter_up[0, 0])


def solution(mesh):
    in_specs = (
        P("section", "tensor"),
        P(None, "tensor"),
        P(),
        P(),
        P("section", None, "tensor"),
        P("section", "tensor", None, None),
        P("section", "tensor", None, None),
    )
    out_specs = P(None, "section", "tensor")
    return jax.shard_map(local, mesh=mesh, in_specs=in_specs, out_specs=out_specs, check_vma=False)
```

```python
import functools

import jax
import jax.numpy as jnp
from jax import lax
from jax.experimental import pallas as pl
from jax.experimental.pallas import tpu as pltpu
from jax.sharding import PartitionSpec as P

TICKS = 2
CAP = 16
NX = 4
B_ROWS = 128
MESH = pl.DeviceIdType.MESH
BF16, F32 = jnp.bfloat16, jnp.float32


def kernel(nz, hidden, arriving, ids, aslot, w_any, d_any, u_any, out, xb, xc, w, d, u, acc, pick, place, lsend, lrecv,
           ssem, rsem, lsem, lora_ssem, lora_rsem):
    nt = NX * nz
    half = nz // 2
    rows = out.shape[1]
    rb, rc = B_ROWS, rows - B_ROWS
    hb, hc = rb // 2, rc // 2
    rank = u.shape[0]
    section = lax.axis_index("section")
    sections = lax.axis_size("section")
    me = lax.axis_index("tensor")
    x, z = me // nz, me % nz
    x_next, x_back = ((x + 1) % NX) * nz + z, ((x + NX - 1) % NX) * nz + z
    z_next, z_back = x * nz + (z + 1) % nz, x * nz + (z + nz - 1) % nz
    s_next, s_back = (section + 1) % sections, (section + sections - 1) % sections
    x_to, z_to = (x_next, x_back), (z_next, z_back)
    z_jump = x * nz + (z + 2) % nz, x * nz + (z + nz - 2) % nz

    locals_ = [
        pltpu.make_async_copy(hidden.at[0:rb], xb.at[0, 0, 0], lsem.at[0]),
        pltpu.make_async_copy(hidden.at[rb:rows], xc.at[0, 0, 0], lsem.at[1]),
        pltpu.make_async_copy(w_any, w, lsem.at[2]),
        pltpu.make_async_copy(d_any, d, lsem.at[3]),
        pltpu.make_async_copy(u_any, u, lsem.at[4]),
    ]
    entry = [
        pltpu.make_async_copy(arriving.at[0:rb], xb.at[1, 0, 0], lsem.at[5]),
        pltpu.make_async_copy(arriving.at[rb:rows], xc.at[1, 0, 0], lsem.at[6]),
    ]
    for c in locals_:
        c.start()

    @pl.when(section == 0)
    def _():
        for c in entry:
            c.start()

    barrier = pltpu.get_barrier_semaphore()
    near = [(section, t) for t in x_to + z_to + z_jump] + [(s_next, me), (s_back, me)]
    for target in near:
        pl.semaphore_signal(barrier, inc=1, device_id=target, device_id_type=MESH)
    pl.semaphore_wait(barrier, len(near))

    sent = []
    stages = half // 2
    n = stages + 1
    EB, EC, FB, FC, XB, XC, NB, NC, SH = (2 * n * i for i in range(9))

    def send(tick, sem, src, dst, to):
        c = pltpu.make_async_remote_copy(
            src_ref=src, dst_ref=dst, send_sem=ssem.at[tick, sem], recv_sem=rsem.at[tick, sem],
            device_id=(section, to), device_id_type=MESH)
        c.start()
        sent.append(c)
        return c

    b_offsets = [0]
    for s in range(stages):
        b_offsets += [2 * s + 1, 2 * s + 2, -2 * s - 1] + ([-2 * s - 2] if s + 1 < stages else [])
    c_offsets = [0]
    for s in range(1, stages):
        c_offsets += [2 * s, -2 * s]
    c_offsets += [half]
    for s in range(stages):
        c_offsets += [2 * s + 1, -2 * s - 1]

    def slot_at(offsets, direction, distance):
        return offsets.index(distance if direction == 0 or distance in (0, half) else -distance)

    def source(x_rel, offset):
        sx = (x + (0, NX - 1, 1, 2)[x_rel]) % NX
        sz = (z + nz - offset) % nz
        return pl.multiple_of((sx * nz + sz) * 128, 128)

    def accumulate(first, count, chunks):
        lhs = jnp.concatenate([c for c, _ in chunks], axis=1)
        base = jnp.concatenate([w[pl.ds(o, 128), :] for _, o in chunks], axis=0)
        down = jnp.concatenate([d[:, pl.ds(o, 128)] for _, o in chunks], axis=1)
        acc[first:first + count, 0:128] += jnp.dot(lhs, base, preferred_element_type=F32)
        acc[first:first + count, 128:128 + rank] += lax.dot_general(lhs, down, (((1,), (1,)), ((), ())), preferred_element_type=F32)

    def compute_b(tick, slots):
        accumulate(0, rb, [(xb[tick, r, s], source(r, b_offsets[s])) for s in slots for r in range(NX)])

    def compute_c(tick, slots):
        accumulate(rb, rc, [(xc[tick, s, r], source(r, c_offsets[s])) for s in slots for r in range(NX)])

    def positions(tick):
        micro = jnp.where(section >= tick, section - tick, sections + tick - 1 - section)
        id_row = ids[micro].astype(F32)
        i0 = lax.broadcasted_iota(jnp.int32, (rows, rows), 0)
        i1 = lax.broadcasted_iota(jnp.int32, (rows, rows), 1)
        id_col = jnp.sum(jnp.where(i0 == i1, id_row, 0.0), axis=1, keepdims=True)
        same = id_col == id_row
        rank_row = jnp.sum(jnp.where(same & (i0 < i1), 1.0, 0.0), axis=0, keepdims=True)
        rank_col = jnp.sum(jnp.where(same & (i1 < i0), 1.0, 0.0), axis=1, keepdims=True)
        named = lax.broadcasted_iota(jnp.int32, (rows, nt), 1).astype(F32) == id_col
        slot_col = jnp.sum(jnp.where(named, aslot[...].astype(F32), 0.0), axis=1, keepdims=True)
        slot_row = jnp.sum(jnp.where(i0 == i1, slot_col, 0.0), axis=0, keepdims=True)
        j = lax.broadcasted_iota(jnp.int32, (CAP, rows), 0).astype(F32)
        pick[tick] = ((slot_row == me.astype(F32)) & (rank_row == j)).astype(BF16)
        q = lax.broadcasted_iota(jnp.int32, (rows, nt * CAP), 1).astype(F32)
        place[tick] = (slot_col * CAP + rank_col == q).astype(BF16)

    def b_group(s):
        return (0, 1) if s == 0 else (4 * s - 3, 4 if s < stages else 3)

    def c_group(s):
        return (0, 1) if s == 0 else (2 * s - 1, 2 if s < stages else 1)

    def tick_work(tick):
        eb, ec, fb, fc, bx, cx, bn, cn = {}, {}, {}, {}, {}, {}, {}, {}

        def express(s):
            for i in (0, 1):
                s0, s1 = slot_at(b_offsets, i, 2 * s), slot_at(b_offsets, i, 2 * s + 2)
                part = pl.ds(i * hb, hb) if s + 1 == stages else pl.ds(0, rb)
                eb[i, s + 1] = send(tick, EB + 2 * s + i, xb.at[tick, 0, s0, part], xb.at[tick, 0, s1, part], z_jump[i])
            for i in (0, 1):
                s0, s1 = slot_at(c_offsets, i, 2 * s), slot_at(c_offsets, i, 2 * s + 2)
                part = pl.ds(i * hc, hc) if s + 1 == stages else pl.ds(0, rc)
                ec[i, s + 1] = send(tick, EC + 2 * s + i, xc.at[tick, s0, 0, part], xc.at[tick, s1, 0, part], z_jump[i])

        def fill_b(s):
            for i in (0, 1):
                s0, s1 = slot_at(b_offsets, i, 2 * s), slot_at(b_offsets, i, 2 * s + 1)
                fb[i, s] = send(tick, FB + 2 * s + i, xb.at[tick, 0, s0], xb.at[tick, 0, s1], z_to[i])

        def fill_c(s):
            for i in (0, 1):
                cn[i, s].wait_recv()
            for i in (0, 1):
                s0, s1 = slot_at(c_offsets, i, 2 * s), slot_at(c_offsets, i, 2 * s + 1)
                fc[i, s] = send(tick, FC + 2 * s + i, xc.at[tick, s0], xc.at[tick, s1], z_to[i])

        def x_b(s):
            part = pl.ds(*b_group(s))
            for i in (0, 1):
                bx[i, s] = send(tick, XB + 2 * s + i, xb.at[tick, 0, part], xb.at[tick, 1 + i, part], x_to[i])

        def x_c(s):
            part = pl.ds(*c_group(s))
            for i in (0, 1):
                cx[i, s] = send(tick, XC + 2 * s + i, xc.at[tick, part, 0], xc.at[tick, part, 1 + i], x_to[i])

        def across_b(s):
            first, count = b_group(s)
            for i in (0, 1):
                bx[i, s].wait_recv()
                if count == 4:
                    part, lines = pl.ds(first + 2 * i, 2), pl.ds(0, rb)
                else:
                    part, lines = pl.ds(first, count), pl.ds(i * hb, hb)
                bn[i, s] = send(tick, NB + 2 * s + i, xb.at[tick, 1 + i, part, lines], xb.at[tick, 3, part, lines], x_to[i])

        def across_c(s):
            first, count = c_group(s)
            for i in (0, 1):
                cx[i, s].wait_recv()
                if count == 2:
                    part, lines = pl.ds(first + i, 1), pl.ds(0, rc)
                else:
                    part, lines = pl.ds(first, 1), pl.ds(i * hc, hc)
                cn[i, s] = send(tick, NC + 2 * s + i, xc.at[tick, part, 1 + i, lines], xc.at[tick, part, 3, lines], x_to[i])

        def arrived(copies, s):
            for i in (0, 1):
                copies[i, s].wait_recv()

        def finish_b(s):
            arrived(bn, s)
            first, count = b_group(s)
            compute_b(tick, range(first, first + count))

        def finish_c(s):
            first, count = c_group(s)
            compute_c(tick, range(first, first + count))

        def finish_odd(s):
            arrived(fc, s)
            compute_c(tick, [slot_at(c_offsets, i, 2 * s + 1) for i in (0, 1)])

        express(0)
        x_c(0)
        fill_b(0)
        x_b(0)
        acc[...] = jnp.zeros_like(acc)
        if tick == 0:
            positions(0)
        across_c(0)
        across_b(0)
        for s in range(1, stages):
            arrived(eb, s)
            arrived(ec, s)
            express(s)
            x_c(s)
            fill_b(s)
            arrived(fb, s - 1)
            x_b(s)
            fill_c(s - 1)
            if tick == 0 and s == 1:
                positions(1)
                for c in locals_[2:]:
                    c.wait()
            finish_c(s - 1)
            finish_b(s - 1)
            across_c(s)
            across_b(s)
            if s > 1:
                finish_odd(s - 2)
        if tick == 0 and stages == 1:
            positions(1)
            for c in locals_[2:]:
                c.wait()
        arrived(eb, stages)
        arrived(ec, stages)
        x_c(stages)
        arrived(fb, stages - 1)
        x_b(stages)
        fill_c(stages - 1)
        finish_c(stages - 1)
        finish_b(stages - 1)
        across_c(stages)
        across_b(stages)
        if stages > 1:
            finish_odd(stages - 2)
        arrived(cn, stages)
        finish_c(stages)
        finish_odd(stages - 1)
        finish_b(stages)

        low = jnp.dot(pick[tick], acc[:, 128:128 + rank].astype(BF16), preferred_element_type=F32).astype(BF16)
        for dx in (2, 1, 3, 0):
            first = ((x + dx) % NX) * nz
            at = pl.multiple_of(first * 128, 128)
            part = jnp.dot(low, u[:, pl.ds(at, nz * 128)], preferred_element_type=F32).astype(BF16)
            for j in range(nz):
                lsend[first + j] = part[:, j * 128:(j + 1) * 128]

            def spread(i, carry):
                dz = (half + (1 - 2 * (i % 2)) * ((i + 1) // 2)) % nz
                to = first + (z + dz) % nz
                pltpu.make_async_remote_copy(
                    src_ref=lsend.at[to], dst_ref=lrecv.at[tick, me], send_sem=lora_ssem.at[tick], recv_sem=lora_rsem.at[tick],
                    device_id=(section, to), device_id_type=MESH).start()
                return carry

            lax.fori_loop(0, nz if dx else nz - 1, spread, 0)
        own = pltpu.make_async_copy(lsend.at[me], lrecv.at[tick, me], lsem.at[7])
        own.start()
        own.wait()
        others = pltpu.make_async_remote_copy(
            src_ref=lsend.at[0:nt - 1], dst_ref=lrecv.at[tick, 0:nt - 1], send_sem=lora_ssem.at[tick], recv_sem=lora_rsem.at[tick],
            device_id=(section, x_next), device_id_type=MESH)
        others.wait_recv()
        lora = jnp.dot(place[tick], lrecv[tick].reshape(nt * CAP, 128), preferred_element_type=F32)
        held = jnp.concatenate([xb[tick, 0, 0], xc[tick, 0, 0]], axis=0).astype(F32)
        out[tick] = (held + acc[:, 0:128] + lora).astype(BF16)
        others.wait_send()

    for c in locals_[:2]:
        c.wait()
    tick_work(0)

    shift = [
        pltpu.make_async_remote_copy(
            src_ref=out.at[0, first:first + count], dst_ref=dst, send_sem=ssem.at[0, SH + i], recv_sem=rsem.at[0, SH + i],
            device_id=(s_next, me), device_id_type=MESH)
        for i, (first, count, dst) in enumerate(((0, rb, xb.at[1, 0, 0]), (rb, rc, xc.at[1, 0, 0])))
    ]

    @pl.when(section + 1 < sections)
    def _():
        for c in shift:
            c.start()

    @pl.when(section > 0)
    def _():
        for c in shift:
            c.wait_recv()

    @pl.when(section == 0)
    def _():
        for c in entry:
            c.wait()

    tick_work(1)

    @pl.when(section + 1 < sections)
    def _():
        for c in shift:
            c.wait_send()

    for c in sent:
        c.wait_send()


def local(hidden, arriving, ids, adapter_slot, base_matrix, adapter_down, adapter_up):
    rows, cols = hidden.shape
    width = base_matrix.shape[1]
    rank = adapter_down.shape[3]
    nt = lax.axis_size("tensor")
    nz = nt // NX
    sems = 16 * (nz // 4 + 1) + 2
    vmem, hbm = pl.BlockSpec(memory_space=pltpu.VMEM), pl.BlockSpec(memory_space=pl.ANY)
    return pl.pallas_call(
        functools.partial(kernel, nz),
        out_shape=jax.ShapeDtypeStruct((TICKS, rows, cols), BF16),
        in_specs=[hbm, hbm, vmem, vmem, hbm, hbm, hbm],
        out_specs=vmem,
        scratch_shapes=[
            pltpu.VMEM((TICKS, NX, nz, B_ROWS, cols), BF16),
            pltpu.VMEM((TICKS, nz, NX, rows - B_ROWS, cols), BF16),
            pltpu.VMEM((width, cols), BF16),
            pltpu.VMEM((rank, width), BF16),
            pltpu.VMEM((rank, width), BF16),
            pltpu.VMEM((rows, cols + rank), F32),
            pltpu.VMEM((TICKS, CAP, rows), BF16),
            pltpu.VMEM((TICKS, rows, nt * CAP), BF16),
            pltpu.VMEM((nt, CAP, cols), BF16),
            pltpu.VMEM((TICKS, nt, CAP, cols), BF16),
            pltpu.SemaphoreType.DMA((TICKS, sems)),
            pltpu.SemaphoreType.DMA((TICKS, sems)),
            pltpu.SemaphoreType.DMA((8,)),
            pltpu.SemaphoreType.DMA((TICKS,)),
            pltpu.SemaphoreType.DMA((TICKS,)),
        ],
        compiler_params=pltpu.CompilerParams(collective_id=0, has_side_effects=True, vmem_limit_bytes=60 * 1024 * 1024),
    )(hidden, arriving, ids.reshape(ids.shape[0], 1, ids.shape[1]), adapter_slot.reshape(1, nt), base_matrix[0], adapter_down[0, 0].T, adapter_up[0, 0])


def solution(mesh):
    in_specs = (
        P("section", "tensor"),
        P(None, "tensor"),
        P(),
        P(),
        P("section", None, "tensor"),
        P("section", "tensor", None, None),
        P("section", "tensor", None, None),
    )
    out_specs = P(None, "section", "tensor")
    return jax.shard_map(local, mesh=mesh, in_specs=in_specs, out_specs=out_specs, check_vma=False)
```

```python
import functools

import jax
import jax.numpy as jnp
from jax import lax
from jax.experimental import pallas as pl
from jax.experimental.pallas import tpu as pltpu
from jax.sharding import PartitionSpec as P

TICKS = 2
CAP = 16
NX = 4
B_ROWS = 96
ORDER = (
    "CE0", "CX0", "BE0", "BP0", "BX0", "CA0", "CE1", "CX1", "BA0", "BE1", "BP1", "BX1", "CF0", "CK0", "CE2", "CX2",
    "CA1", "BK0", "BE2", "BP2", "BX2", "BA1", "CA2", "CG0", "CF1", "CK1", "CE3", "CX3", "BA2", "BE3", "BP3", "BX3",
    "BK1", "CF2", "CK2", "CA3", "CG1", "BK2", "CE4", "CX4", "BE4", "BX4", "BA3", "CF3", "CK3", "CA4", "CG2", "BA4",
    "BK3", "CK4", "CG3", "BK4",
)
MESH = pl.DeviceIdType.MESH
BF16, F32 = jnp.bfloat16, jnp.float32


def kernel(nz, hidden, arriving, ids, aslot, w_any, d_any, u_any, out, xb, xc, w, d, u, acc, pick, place, lsend, lrecv,
           ssem, rsem, lsem, lora_ssem, lora_rsem):
    nt = NX * nz
    half = nz // 2
    rows = out.shape[1]
    rb, rc = B_ROWS, rows - B_ROWS
    hb, hc = rb // 2, rc // 2
    rank = u.shape[0]
    section = lax.axis_index("section")
    sections = lax.axis_size("section")
    me = lax.axis_index("tensor")
    x, z = me // nz, me % nz
    x_next, x_back = ((x + 1) % NX) * nz + z, ((x + NX - 1) % NX) * nz + z
    z_next, z_back = x * nz + (z + 1) % nz, x * nz + (z + nz - 1) % nz
    s_next, s_back = (section + 1) % sections, (section + sections - 1) % sections
    x_to, z_to = (x_next, x_back), (z_next, z_back)
    z_jump = x * nz + (z + 2) % nz, x * nz + (z + nz - 2) % nz

    locals_ = [
        pltpu.make_async_copy(hidden.at[0:rb], xb.at[0, 0, 0], lsem.at[0]),
        pltpu.make_async_copy(hidden.at[rb:rows], xc.at[0, 0, 0], lsem.at[1]),
        pltpu.make_async_copy(w_any, w, lsem.at[2]),
        pltpu.make_async_copy(d_any, d, lsem.at[3]),
        pltpu.make_async_copy(u_any, u, lsem.at[4]),
    ]
    entry = [
        pltpu.make_async_copy(arriving.at[0:rb], xb.at[1, 0, 0], lsem.at[5]),
        pltpu.make_async_copy(arriving.at[rb:rows], xc.at[1, 0, 0], lsem.at[6]),
    ]
    for c in locals_:
        c.start()

    @pl.when(section == 0)
    def _():
        for c in entry:
            c.start()

    barrier = pltpu.get_barrier_semaphore()
    senders = [(section, t) for t in x_to + z_to + z_jump] + [(s_back, me)]
    for target in senders:
        pl.semaphore_signal(barrier, inc=1, device_id=target, device_id_type=MESH)
    pl.semaphore_wait(barrier, len(senders))

    sent = []
    stages = half // 2
    n = stages + 1
    EB, EC, FB, FC, XB, XC, NB, NC, SH = (2 * n * i for i in range(9))
    later = []

    def send(tick, sem, src, dst, to, first_line=None):
        c = pltpu.make_async_remote_copy(
            src_ref=src, dst_ref=dst, send_sem=ssem.at[tick, sem], recv_sem=rsem.at[tick, sem],
            device_id=(section, to), device_id_type=MESH)
        if tick == 0 or first_line is None:
            c.start()
            sent.append(c)
            return c
        lines = src.shape[-2]
        ahead = pltpu.make_async_remote_copy(
            src_ref=out.at[tick - 1, first_line:first_line + lines], dst_ref=dst, send_sem=ssem.at[tick - 1, SH + 2 + len(later) // 2],
            recv_sem=rsem.at[tick, sem], device_id=(s_next, to), device_id_type=MESH)

        @pl.when(section + 1 < sections)
        def _():
            ahead.start()

        @pl.when(section == 0)
        def _():
            c.start()

        later.extend([(section + 1 < sections, ahead), (section == 0, c)])
        return c

    b_offsets = [0]
    for s in range(stages):
        b_offsets += [2 * s + 1, 2 * s + 2, -2 * s - 1] + ([-2 * s - 2] if s + 1 < stages else [])
    c_offsets = [0]
    for s in range(1, stages):
        c_offsets += [2 * s, -2 * s]
    c_offsets += [half]
    for s in range(stages):
        c_offsets += [2 * s + 1, -2 * s - 1]

    def slot_at(offsets, direction, distance):
        return offsets.index(distance if direction == 0 or distance in (0, half) else -distance)

    def source(x_rel, offset):
        sx = (x + (0, NX - 1, 1, 2)[x_rel]) % NX
        sz = (z + nz - offset) % nz
        return pl.multiple_of((sx * nz + sz) * 128, 128)

    def accumulate(first, count, chunks):
        lhs = jnp.concatenate([c for c, _ in chunks], axis=1)
        base = jnp.concatenate([w[pl.ds(o, 128), :] for _, o in chunks], axis=0)
        down = jnp.concatenate([d[:, pl.ds(o, 128)] for _, o in chunks], axis=1)
        acc[first:first + count, 0:128] += jnp.dot(lhs, base, preferred_element_type=F32)
        acc[first:first + count, 128:128 + rank] += lax.dot_general(lhs, down, (((1,), (1,)), ((), ())), preferred_element_type=F32)

    def compute_b(tick, slots):
        accumulate(0, rb, [(xb[tick, r, s], source(r, b_offsets[s])) for s in slots for r in range(NX)])

    def compute_c(tick, slots):
        accumulate(rb, rc, [(xc[tick, s, r], source(r, c_offsets[s])) for s in slots for r in range(NX)])

    def positions(tick):
        micro = jnp.where(section >= tick, section - tick, sections + tick - 1 - section)
        id_row = ids[micro].astype(F32)
        i0 = lax.broadcasted_iota(jnp.int32, (rows, rows), 0)
        i1 = lax.broadcasted_iota(jnp.int32, (rows, rows), 1)
        id_col = jnp.sum(jnp.where(i0 == i1, id_row, 0.0), axis=1, keepdims=True)
        same = id_col == id_row
        rank_row = jnp.sum(jnp.where(same & (i0 < i1), 1.0, 0.0), axis=0, keepdims=True)
        rank_col = jnp.sum(jnp.where(same & (i1 < i0), 1.0, 0.0), axis=1, keepdims=True)
        named = lax.broadcasted_iota(jnp.int32, (rows, nt), 1).astype(F32) == id_col
        slot_col = jnp.sum(jnp.where(named, aslot[...].astype(F32), 0.0), axis=1, keepdims=True)
        slot_row = jnp.sum(jnp.where(i0 == i1, slot_col, 0.0), axis=0, keepdims=True)
        j = lax.broadcasted_iota(jnp.int32, (CAP, rows), 0).astype(F32)
        pick[tick] = ((slot_row == me.astype(F32)) & (rank_row == j)).astype(BF16)
        q = lax.broadcasted_iota(jnp.int32, (rows, nt * CAP), 1).astype(F32)
        place[tick] = (slot_col * CAP + rank_col == q).astype(BF16)

    def b_group(s):
        return (0, 1) if s == 0 else (4 * s - 3, 4 if s < stages else 3)

    def c_group(s):
        return (0, 1) if s == 0 else (2 * s - 1, 2 if s < stages else 1)

    def tick_work(tick):
        eb, ec, fb, fc, bx, cx, bn, cn = {}, {}, {}, {}, {}, {}, {}, {}

        def express_b(s):
            if s > 0:
                arrived(eb, s)
            for i in (0, 1) if s < stages else ():
                s0, s1 = slot_at(b_offsets, i, 2 * s), slot_at(b_offsets, i, 2 * s + 2)
                part = pl.ds(i * hb, hb) if s + 1 == stages else pl.ds(0, rb)
                eb[i, s + 1] = send(tick, EB + 2 * s + i, xb.at[tick, 0, s0, part], xb.at[tick, 0, s1, part], z_jump[i],
                                    first_line=None if s else i * hb if s + 1 == stages else 0)

        def express_c(s):
            if s > 0:
                arrived(ec, s)
            for i in (0, 1) if s < stages else ():
                s0, s1 = slot_at(c_offsets, i, 2 * s), slot_at(c_offsets, i, 2 * s + 2)
                part = pl.ds(i * hc, hc) if s + 1 == stages else pl.ds(0, rc)
                ec[i, s + 1] = send(tick, EC + 2 * s + i, xc.at[tick, s0, 0, part], xc.at[tick, s1, 0, part], z_jump[i],
                                    first_line=None if s else rb + (i * hc if s + 1 == stages else 0))

        def fill_b(s):
            for i in (0, 1):
                s0, s1 = slot_at(b_offsets, i, 2 * s), slot_at(b_offsets, i, 2 * s + 1)
                fb[i, s] = send(tick, FB + 2 * s + i, xb.at[tick, 0, s0], xb.at[tick, 0, s1], z_to[i], first_line=None if s else 0)

        def fill_c(s):
            arrived(cn, s)
            for i in (0, 1):
                s0, s1 = slot_at(c_offsets, i, 2 * s), slot_at(c_offsets, i, 2 * s + 1)
                fc[i, s] = send(tick, FC + 2 * s + i, xc.at[tick, s0], xc.at[tick, s1], z_to[i])

        def x_b(s):
            if s > 0:
                arrived(fb, s - 1)
            part = pl.ds(*b_group(s)) if s else 0
            for i in (0, 1):
                bx[i, s] = send(tick, XB + 2 * s + i, xb.at[tick, 0, part], xb.at[tick, 1 + i, part], x_to[i], first_line=None if s else 0)

        def x_c(s):
            part = pl.ds(*c_group(s)) if s else 0
            for i in (0, 1):
                cx[i, s] = send(tick, XC + 2 * s + i, xc.at[tick, part, 0], xc.at[tick, part, 1 + i], x_to[i], first_line=None if s else rb)

        def across_b(s):
            first, count = b_group(s)
            for i in (0, 1):
                bx[i, s].wait_recv()
                if count == 4:
                    part, lines = pl.ds(first + 2 * i, 2), pl.ds(0, rb)
                else:
                    part, lines = pl.ds(first, count), pl.ds(i * hb, hb)
                bn[i, s] = send(tick, NB + 2 * s + i, xb.at[tick, 1 + i, part, lines], xb.at[tick, 3, part, lines], x_to[i])

        def across_c(s):
            first, count = c_group(s)
            for i in (0, 1):
                cx[i, s].wait_recv()
                if count == 2:
                    part, lines = pl.ds(first + i, 1), pl.ds(0, rc)
                else:
                    part, lines = pl.ds(first, 1), pl.ds(i * hc, hc)
                cn[i, s] = send(tick, NC + 2 * s + i, xc.at[tick, part, 1 + i, lines], xc.at[tick, part, 3, lines], x_to[i])

        def arrived(copies, s):
            for i in (0, 1):
                copies[i, s].wait_recv()

        def finish_b(s):
            arrived(bn, s)
            first, count = b_group(s)
            compute_b(tick, range(first, first + count))

        def finish_c(s):
            if s == stages:
                arrived(cn, s)
            first, count = c_group(s)
            compute_c(tick, range(first, first + count))

        def finish_odd(s):
            arrived(fc, s)
            compute_c(tick, [slot_at(c_offsets, i, 2 * s + 1) for i in (0, 1)])

        tasks = dict(BE=express_b, BP=fill_b, BX=x_b, BA=across_b, BK=finish_b, CE=express_c, CX=x_c, CA=across_c, CF=fill_c, CK=finish_c,
                     CG=finish_odd)
        if stages == 4:
            steps = ORDER
        else:
            steps = [k + str(s) for s in range(stages) for k in ("CE", "CX", "BE", "BP", "BX", "CA", "CF", "BA", "CK", "BK")]
            steps += [k + str(stages) for k in ("CE", "CX", "BE", "BX", "CA", "CK", "BA", "BK")]
            steps += ["CG" + str(s) for s in range(stages)]
        acc[...] = jnp.zeros_like(acc)
        loaded = False
        for at, step in enumerate(steps):
            if tick == 0 and at == 5:
                positions(0)
            if not loaded and step[1] in "FKG":
                if tick == 0:
                    for c in locals_[2:]:
                        c.wait()
                    positions(1)
                else:
                    entered()
                loaded = True
            tasks[step[:2]](int(step[2:]))
            if tick == 1 and at == 4:
                @pl.when(section + 1 < sections)
                def _():
                    for c in shift:
                        c.start()

        low = jnp.dot(pick[tick], acc[:, 128:128 + rank].astype(BF16), preferred_element_type=F32).astype(BF16)
        for dx in (2, 1, 3, 0):
            first = ((x + dx) % NX) * nz
            at = pl.multiple_of(first * 128, 128)
            part = jnp.dot(low, u[:, pl.ds(at, nz * 128)], preferred_element_type=F32).astype(BF16)
            for j in range(nz):
                lsend[first + j] = part[:, j * 128:(j + 1) * 128]

            def spread(i, carry):
                dz = (half + (1 - 2 * (i % 2)) * ((i + 1) // 2)) % nz
                to = first + (z + dz) % nz
                pltpu.make_async_remote_copy(
                    src_ref=lsend.at[to], dst_ref=lrecv.at[tick, me], send_sem=lora_ssem.at[tick], recv_sem=lora_rsem.at[tick],
                    device_id=(section, to), device_id_type=MESH).start()
                return carry

            lax.fori_loop(0, nz if dx else nz - 1, spread, 0)
        own = pltpu.make_async_copy(lsend.at[me], lrecv.at[tick, me], lsem.at[7])
        own.start()
        own.wait()
        others = pltpu.make_async_remote_copy(
            src_ref=lsend.at[0:nt - 1], dst_ref=lrecv.at[tick, 0:nt - 1], send_sem=lora_ssem.at[tick], recv_sem=lora_rsem.at[tick],
            device_id=(section, x_next), device_id_type=MESH)
        others.wait_recv()
        lora = jnp.dot(place[tick], lrecv[tick].reshape(nt * CAP, 128), preferred_element_type=F32)
        held = jnp.concatenate([xb[tick, 0, 0], xc[tick, 0, 0]], axis=0).astype(F32)
        out[tick] = (held + acc[:, 0:128] + lora).astype(BF16)
        others.wait_send()

    shift = [
        pltpu.make_async_remote_copy(
            src_ref=out.at[0, first:first + count], dst_ref=dst, send_sem=ssem.at[0, SH + i], recv_sem=rsem.at[0, SH + i],
            device_id=(s_next, me), device_id_type=MESH)
        for i, (first, count, dst) in enumerate(((0, rb, xb.at[1, 0, 0]), (rb, rc, xc.at[1, 0, 0])))
    ]

    def entered():
        @pl.when(section > 0)
        def _():
            for c in shift:
                c.wait_recv()

    for c in locals_[:2]:
        c.wait()
    tick_work(0)

    @pl.when(section == 0)
    def _():
        for c in entry:
            c.wait()

    tick_work(1)

    @pl.when(section + 1 < sections)
    def _():
        for c in shift:
            c.wait_send()

    for c in sent:
        c.wait_send()
    for some, c in later:
        @pl.when(some)
        def _():
            c.wait_send()


def local(hidden, arriving, ids, adapter_slot, base_matrix, adapter_down, adapter_up):
    rows, cols = hidden.shape
    width = base_matrix.shape[1]
    rank = adapter_down.shape[3]
    nt = lax.axis_size("tensor")
    nz = nt // NX
    sems = 16 * (nz // 4 + 1) + 12
    vmem, hbm = pl.BlockSpec(memory_space=pltpu.VMEM), pl.BlockSpec(memory_space=pl.ANY)
    return pl.pallas_call(
        functools.partial(kernel, nz),
        out_shape=jax.ShapeDtypeStruct((TICKS, rows, cols), BF16),
        in_specs=[hbm, hbm, vmem, vmem, hbm, hbm, hbm],
        out_specs=vmem,
        scratch_shapes=[
            pltpu.VMEM((TICKS, NX, nz, B_ROWS, cols), BF16),
            pltpu.VMEM((TICKS, nz, NX, rows - B_ROWS, cols), BF16),
            pltpu.VMEM((width, cols), BF16),
            pltpu.VMEM((rank, width), BF16),
            pltpu.VMEM((rank, width), BF16),
            pltpu.VMEM((rows, cols + rank), F32),
            pltpu.VMEM((TICKS, CAP, rows), BF16),
            pltpu.VMEM((TICKS, rows, nt * CAP), BF16),
            pltpu.VMEM((nt, CAP, cols), BF16),
            pltpu.VMEM((TICKS, nt, CAP, cols), BF16),
            pltpu.SemaphoreType.DMA((TICKS, sems)),
            pltpu.SemaphoreType.DMA((TICKS, sems)),
            pltpu.SemaphoreType.DMA((8,)),
            pltpu.SemaphoreType.DMA((TICKS,)),
            pltpu.SemaphoreType.DMA((TICKS,)),
        ],
        compiler_params=pltpu.CompilerParams(collective_id=0, has_side_effects=True, vmem_limit_bytes=60 * 1024 * 1024),
    )(hidden, arriving, ids.reshape(ids.shape[0], 1, ids.shape[1]), adapter_slot.reshape(1, nt), base_matrix[0], adapter_down[0, 0].T, adapter_up[0, 0])


def solution(mesh):
    in_specs = (
        P("section", "tensor"),
        P(None, "tensor"),
        P(),
        P(),
        P("section", None, "tensor"),
        P("section", "tensor", None, None),
        P("section", "tensor", None, None),
    )
    out_specs = P(None, "section", "tensor")
    return jax.shard_map(local, mesh=mesh, in_specs=in_specs, out_specs=out_specs, check_vma=False)
```

```python
import functools

import jax
import jax.numpy as jnp
from jax import lax
from jax.experimental import pallas as pl
from jax.experimental.pallas import tpu as pltpu
from jax.sharding import PartitionSpec as P

TICKS = 2
CAP = 16
NX = 4
B_ROWS = 96
ORDER = (
    "CE0", "CX0", "BE0", "BP0", "BX0", "CA0", "CE1", "CX1", "BA0", "BE1", "BP1", "BX1", "CF0", "CK0", "CE2", "CX2",
    "CA1", "BK0", "BE2", "BP2", "BX2", "BA1", "CA2", "CG0", "CF1", "CK1", "CE3", "CX3", "BA2", "BE3", "BP3", "BX3",
    "BK1", "CF2", "CK2", "CA3", "CG1", "BK2", "CE4", "CX4", "BE4", "BX4", "BA3", "CF3", "CK3", "CA4", "CG2", "BA4",
    "BK3", "CK4", "CG3", "BK4",
)
MESH = pl.DeviceIdType.MESH
BF16, F32 = jnp.bfloat16, jnp.float32


def kernel(nz, hidden, arriving, ids, aslot, w_any, d_any, u_any, out, xb, xc, w, d, u, acc, pick, place, lsend, lrecv,
           ssem, rsem, lsem, lora_ssem, lora_rsem):
    nt = NX * nz
    half = nz // 2
    rows = out.shape[1]
    rb, rc = B_ROWS, rows - B_ROWS
    hb, hc = rb // 2, rc // 2
    rank = u.shape[0]
    section = lax.axis_index("section")
    sections = lax.axis_size("section")
    me = lax.axis_index("tensor")
    x, z = me // nz, me % nz
    x_next, x_back = ((x + 1) % NX) * nz + z, ((x + NX - 1) % NX) * nz + z
    z_next, z_back = x * nz + (z + 1) % nz, x * nz + (z + nz - 1) % nz
    s_next, s_back = (section + 1) % sections, (section + sections - 1) % sections
    x_to, z_to = (x_next, x_back), (z_next, z_back)
    z_jump = x * nz + (z + 2) % nz, x * nz + (z + nz - 2) % nz

    barrier = pltpu.get_barrier_semaphore()
    senders = [(section, t) for t in x_to + z_to + z_jump] + [(s_back, me)]
    for target in senders:
        pl.semaphore_signal(barrier, inc=1, device_id=target, device_id_type=MESH)

    locals_ = [
        pltpu.make_async_copy(hidden.at[0:rb], xb.at[0, 0, 0], lsem.at[0]),
        pltpu.make_async_copy(hidden.at[rb:rows], xc.at[0, 0, 0], lsem.at[1]),
        pltpu.make_async_copy(w_any, w, lsem.at[2]),
        pltpu.make_async_copy(d_any, d, lsem.at[3]),
        pltpu.make_async_copy(u_any, u, lsem.at[4]),
    ]
    entry = [
        pltpu.make_async_copy(arriving.at[0:rb], xb.at[1, 0, 0], lsem.at[5]),
        pltpu.make_async_copy(arriving.at[rb:rows], xc.at[1, 0, 0], lsem.at[6]),
    ]
    for c in locals_:
        c.start()

    @pl.when(section == 0)
    def _():
        for c in entry:
            c.start()

    pl.semaphore_wait(barrier, len(senders))

    sent = []
    stages = half // 2
    n = stages + 1
    EB, EC, FB, FC, XB, XC, NB, NC, SH = (2 * n * i for i in range(9))
    later = []

    def send(tick, sem, src, dst, to, first_line=None):
        c = pltpu.make_async_remote_copy(
            src_ref=src, dst_ref=dst, send_sem=ssem.at[tick, sem], recv_sem=rsem.at[tick, sem],
            device_id=(section, to), device_id_type=MESH)
        if tick == 0 or first_line is None:
            c.start()
            sent.append(c)
            return c
        lines = src.shape[-2]
        ahead = pltpu.make_async_remote_copy(
            src_ref=out.at[tick - 1, first_line:first_line + lines], dst_ref=dst, send_sem=ssem.at[tick - 1, SH + 2 + len(later) // 2],
            recv_sem=rsem.at[tick, sem], device_id=(s_next, to), device_id_type=MESH)

        @pl.when(section + 1 < sections)
        def _():
            ahead.start()

        @pl.when(section == 0)
        def _():
            c.start()

        later.extend([(section + 1 < sections, ahead), (section == 0, c)])
        return c

    b_offsets = [0]
    for s in range(stages):
        b_offsets += [2 * s + 1, 2 * s + 2, -2 * s - 1] + ([-2 * s - 2] if s + 1 < stages else [])
    c_offsets = [0]
    for s in range(1, stages):
        c_offsets += [2 * s, -2 * s]
    c_offsets += [half]
    for s in range(stages):
        c_offsets += [2 * s + 1, -2 * s - 1]

    def slot_at(offsets, direction, distance):
        return offsets.index(distance if direction == 0 or distance in (0, half) else -distance)

    def source(x_rel, offset):
        sx = (x + (0, NX - 1, 1, 2)[x_rel]) % NX
        sz = (z + nz - offset) % nz
        return pl.multiple_of((sx * nz + sz) * 128, 128)

    def accumulate(first, count, chunks):
        lhs = jnp.concatenate([c for c, _ in chunks], axis=1)
        base = jnp.concatenate([w[pl.ds(o, 128), :] for _, o in chunks], axis=0)
        down = jnp.concatenate([d[:, pl.ds(o, 128)] for _, o in chunks], axis=1)
        acc[first:first + count, 0:128] += jnp.dot(lhs, base, preferred_element_type=F32)
        acc[first:first + count, 128:128 + rank] += lax.dot_general(lhs, down, (((1,), (1,)), ((), ())), preferred_element_type=F32)

    def compute_b(tick, slots):
        accumulate(0, rb, [(xb[tick, r, s], source(r, b_offsets[s])) for s in slots for r in range(NX)])

    def compute_c(tick, slots):
        accumulate(rb, rc, [(xc[tick, s, r], source(r, c_offsets[s])) for s in slots for r in range(NX)])

    def positions(tick):
        micro = jnp.where(section >= tick, section - tick, sections + tick - 1 - section)
        id_row = ids[micro].astype(F32)
        i0 = lax.broadcasted_iota(jnp.int32, (rows, rows), 0)
        i1 = lax.broadcasted_iota(jnp.int32, (rows, rows), 1)
        id_col = jnp.sum(jnp.where(i0 == i1, id_row, 0.0), axis=1, keepdims=True)
        same = id_col == id_row
        rank_row = jnp.sum(jnp.where(same & (i0 < i1), 1.0, 0.0), axis=0, keepdims=True)
        rank_col = jnp.sum(jnp.where(same & (i1 < i0), 1.0, 0.0), axis=1, keepdims=True)
        named = lax.broadcasted_iota(jnp.int32, (rows, nt), 1).astype(F32) == id_col
        slot_col = jnp.sum(jnp.where(named, aslot[...].astype(F32), 0.0), axis=1, keepdims=True)
        slot_row = jnp.sum(jnp.where(i0 == i1, slot_col, 0.0), axis=0, keepdims=True)
        j = lax.broadcasted_iota(jnp.int32, (CAP, rows), 0).astype(F32)
        pick[tick] = ((slot_row == me.astype(F32)) & (rank_row == j)).astype(BF16)
        q = lax.broadcasted_iota(jnp.int32, (rows, nt * CAP), 1).astype(F32)
        place[tick] = (slot_col * CAP + rank_col == q).astype(BF16)

    def b_group(s):
        return (0, 1) if s == 0 else (4 * s - 3, 4 if s < stages else 3)

    def c_group(s):
        return (0, 1) if s == 0 else (2 * s - 1, 2 if s < stages else 1)

    def tick_work(tick):
        eb, ec, fb, fc, bx, cx, bn, cn = {}, {}, {}, {}, {}, {}, {}, {}

        def express_b(s):
            if s > 0:
                arrived(eb, s)
            for i in (0, 1) if s < stages else ():
                s0, s1 = slot_at(b_offsets, i, 2 * s), slot_at(b_offsets, i, 2 * s + 2)
                part = pl.ds(i * hb, hb) if s + 1 == stages else pl.ds(0, rb)
                eb[i, s + 1] = send(tick, EB + 2 * s + i, xb.at[tick, 0, s0, part], xb.at[tick, 0, s1, part], z_jump[i],
                                    first_line=None if s else i * hb if s + 1 == stages else 0)

        def express_c(s):
            if s > 0:
                arrived(ec, s)
            for i in (0, 1) if s < stages else ():
                s0, s1 = slot_at(c_offsets, i, 2 * s), slot_at(c_offsets, i, 2 * s + 2)
                part = pl.ds(i * hc, hc) if s + 1 == stages else pl.ds(0, rc)
                ec[i, s + 1] = send(tick, EC + 2 * s + i, xc.at[tick, s0, 0, part], xc.at[tick, s1, 0, part], z_jump[i],
                                    first_line=None if s else rb + (i * hc if s + 1 == stages else 0))

        def fill_b(s):
            for i in (0, 1):
                s0, s1 = slot_at(b_offsets, i, 2 * s), slot_at(b_offsets, i, 2 * s + 1)
                fb[i, s] = send(tick, FB + 2 * s + i, xb.at[tick, 0, s0], xb.at[tick, 0, s1], z_to[i], first_line=None if s else 0)

        def fill_c(s):
            arrived(cn, s)
            for i in (0, 1):
                s0, s1 = slot_at(c_offsets, i, 2 * s), slot_at(c_offsets, i, 2 * s + 1)
                fc[i, s] = send(tick, FC + 2 * s + i, xc.at[tick, s0], xc.at[tick, s1], z_to[i])

        def x_b(s):
            if s > 0:
                arrived(fb, s - 1)
            part = pl.ds(*b_group(s)) if s else 0
            for i in (0, 1):
                bx[i, s] = send(tick, XB + 2 * s + i, xb.at[tick, 0, part], xb.at[tick, 1 + i, part], x_to[i], first_line=None if s else 0)

        def x_c(s):
            part = pl.ds(*c_group(s)) if s else 0
            for i in (0, 1):
                cx[i, s] = send(tick, XC + 2 * s + i, xc.at[tick, part, 0], xc.at[tick, part, 1 + i], x_to[i], first_line=None if s else rb)

        def across_b(s):
            first, count = b_group(s)
            for i in (0, 1):
                bx[i, s].wait_recv()
                if count == 4:
                    part, lines = pl.ds(first + 2 * i, 2), pl.ds(0, rb)
                else:
                    part, lines = pl.ds(first, count), pl.ds(i * hb, hb)
                bn[i, s] = send(tick, NB + 2 * s + i, xb.at[tick, 1 + i, part, lines], xb.at[tick, 3, part, lines], x_to[i])

        def across_c(s):
            first, count = c_group(s)
            for i in (0, 1):
                cx[i, s].wait_recv()
                if count == 2:
                    part, lines = pl.ds(first + i, 1), pl.ds(0, rc)
                else:
                    part, lines = pl.ds(first, 1), pl.ds(i * hc, hc)
                cn[i, s] = send(tick, NC + 2 * s + i, xc.at[tick, part, 1 + i, lines], xc.at[tick, part, 3, lines], x_to[i])

        def arrived(copies, s):
            for i in (0, 1):
                copies[i, s].wait_recv()

        def finish_b(s):
            arrived(bn, s)
            first, count = b_group(s)
            compute_b(tick, range(first, first + count))

        def finish_c(s):
            if s == stages:
                arrived(cn, s)
            first, count = c_group(s)
            compute_c(tick, range(first, first + count))

        def finish_odd(s):
            arrived(fc, s)
            compute_c(tick, [slot_at(c_offsets, i, 2 * s + 1) for i in (0, 1)])

        tasks = dict(BE=express_b, BP=fill_b, BX=x_b, BA=across_b, BK=finish_b, CE=express_c, CX=x_c, CA=across_c, CF=fill_c, CK=finish_c,
                     CG=finish_odd)
        if stages == 4:
            steps = ORDER
        else:
            steps = [k + str(s) for s in range(stages) for k in ("CE", "CX", "BE", "BP", "BX", "CA", "CF", "BA", "CK", "BK")]
            steps += [k + str(stages) for k in ("CE", "CX", "BE", "BX", "CA", "CK", "BA", "BK")]
            steps += ["CG" + str(s) for s in range(stages)]
        loaded = False
        for at, step in enumerate(steps):
            if at == 5:
                acc[...] = jnp.zeros_like(acc)
                if tick == 0:
                    positions(0)
            if not loaded and step[1] in "FKG":
                if tick == 0:
                    for c in locals_[2:]:
                        c.wait()
                else:
                    entered()
                loaded = True
            tasks[step[:2]](int(step[2:]))
            if tick == 1 and at == 4:
                @pl.when(section + 1 < sections)
                def _():
                    for c in shift:
                        c.start()

        low = jnp.dot(pick[tick], acc[:, 128:128 + rank].astype(BF16), preferred_element_type=F32).astype(BF16)
        for dx in (2, 1, 3, 0):
            first = ((x + dx) % NX) * nz
            at = pl.multiple_of(first * 128, 128)
            part = jnp.dot(low, u[:, pl.ds(at, nz * 128)], preferred_element_type=F32).astype(BF16)
            for j in range(nz):
                lsend[first + j] = part[:, j * 128:(j + 1) * 128]

            def spread(dz):
                to = first + (z + dz) % nz
                pltpu.make_async_remote_copy(
                    src_ref=lsend.at[to], dst_ref=lrecv.at[tick, me], send_sem=lora_ssem.at[tick], recv_sem=lora_rsem.at[tick],
                    device_id=(section, to), device_id_type=MESH).start()

            def pair(i, carry):
                spread(half - i)
                spread(half + i)
                return carry

            spread(half)
            lax.fori_loop(1, half, pair, 0)
            if dx:
                spread(0)
        own = pltpu.make_async_copy(lsend.at[me], lrecv.at[tick, me], lsem.at[7])
        own.start()
        own.wait()
        others = pltpu.make_async_remote_copy(
            src_ref=lsend.at[0:nt - 1], dst_ref=lrecv.at[tick, 0:nt - 1], send_sem=lora_ssem.at[tick], recv_sem=lora_rsem.at[tick],
            device_id=(section, x_next), device_id_type=MESH)
        if tick + 1 < TICKS:
            positions(tick + 1)
        others.wait_recv()
        lora = jnp.dot(place[tick], lrecv[tick].reshape(nt * CAP, 128), preferred_element_type=F32)
        held = jnp.concatenate([xb[tick, 0, 0], xc[tick, 0, 0]], axis=0).astype(F32)
        out[tick] = (held + acc[:, 0:128] + lora).astype(BF16)
        others.wait_send()

    shift = [
        pltpu.make_async_remote_copy(
            src_ref=out.at[0, first:first + count], dst_ref=dst, send_sem=ssem.at[0, SH + i], recv_sem=rsem.at[0, SH + i],
            device_id=(s_next, me), device_id_type=MESH)
        for i, (first, count, dst) in enumerate(((0, rb, xb.at[1, 0, 0]), (rb, rc, xc.at[1, 0, 0])))
    ]

    def entered():
        @pl.when(section > 0)
        def _():
            for c in shift:
                c.wait_recv()

    for c in locals_[:2]:
        c.wait()
    tick_work(0)

    @pl.when(section == 0)
    def _():
        for c in entry:
            c.wait()

    tick_work(1)

    @pl.when(section + 1 < sections)
    def _():
        for c in shift:
            c.wait_send()

    for c in sent:
        c.wait_send()
    for some, c in later:
        @pl.when(some)
        def _():
            c.wait_send()


def local(hidden, arriving, ids, adapter_slot, base_matrix, adapter_down, adapter_up):
    rows, cols = hidden.shape
    width = base_matrix.shape[1]
    rank = adapter_down.shape[3]
    nt = lax.axis_size("tensor")
    nz = nt // NX
    sems = 16 * (nz // 4 + 1) + 12
    vmem, hbm = pl.BlockSpec(memory_space=pltpu.VMEM), pl.BlockSpec(memory_space=pl.ANY)
    return pl.pallas_call(
        functools.partial(kernel, nz),
        out_shape=pltpu.VMEM((TICKS, rows, cols), BF16),
        in_specs=[hbm, hbm, vmem, vmem, hbm, hbm, hbm],
        out_specs=vmem,
        scratch_shapes=[
            pltpu.VMEM((TICKS, NX, nz, B_ROWS, cols), BF16),
            pltpu.VMEM((TICKS, nz, NX, rows - B_ROWS, cols), BF16),
            pltpu.VMEM((width, cols), BF16),
            pltpu.VMEM((rank, width), BF16),
            pltpu.VMEM((rank, width), BF16),
            pltpu.VMEM((rows, cols + rank), F32),
            pltpu.VMEM((TICKS, CAP, rows), BF16),
            pltpu.VMEM((TICKS, rows, nt * CAP), BF16),
            pltpu.VMEM((nt, CAP, cols), BF16),
            pltpu.VMEM((TICKS, nt, CAP, cols), BF16),
            pltpu.SemaphoreType.DMA((TICKS, sems)),
            pltpu.SemaphoreType.DMA((TICKS, sems)),
            pltpu.SemaphoreType.DMA((8,)),
            pltpu.SemaphoreType.DMA((TICKS,)),
            pltpu.SemaphoreType.DMA((TICKS,)),
        ],
        compiler_params=pltpu.CompilerParams(collective_id=0, has_side_effects=True, vmem_limit_bytes=60 * 1024 * 1024),
    )(hidden, arriving, ids.reshape(ids.shape[0], 1, ids.shape[1]), adapter_slot.reshape(1, nt), base_matrix[0], adapter_down[0, 0].T, adapter_up[0, 0])


def solution(mesh):
    in_specs = (
        P("section", "tensor"),
        P(None, "tensor"),
        P(),
        P(),
        P("section", None, "tensor"),
        P("section", "tensor", None, None),
        P("section", "tensor", None, None),
    )
    out_specs = P(None, "section", "tensor")
    return jax.shard_map(local, mesh=mesh, in_specs=in_specs, out_specs=out_specs, check_vma=False)
```
